256 devices in a mesh: dp: 64 (over x_lo, z, y), tensor: 4 (over x_hi, core).
Axes of the slice: x: 4 (x_hi: 2, x_lo: 2; x = x_hi * 2 + x_lo), y: 4, z: 8, core: 2. Of those that a mesh axis runs over, the one named last changes fastest.
Arguments:
- hidden: bfloat16 [16384, 3072], P('dp'), may hold values from -6 to 6
- branch: bfloat16 [16384, 3072], P('dp'), may hold values from -6 to 6
- up_grad: bfloat16 [16384, 3072], P('dp', 'tensor'), may hold values from -6 to 6
- timesteps: int32 [4], replicated, may hold values from 0 to 999
- w_time: bfloat16 [256, 3072], replicated, may hold values from -0.375 to 0.375
- w_gate: bfloat16 [3072, 3072], P('dp', 'tensor'), may hold values from -0.109375 to 0.109375
- w_in: bfloat16 [3072, 2048], P('dp', 'tensor'), may hold values from -0.109375 to 0.109375
- w_mid: bfloat16 [2048, 2048], P('tensor', 'dp'), may hold values from -0.125 to 0.125
- w_out: bfloat16 [2048, 1536], P('dp', 'tensor'), may hold values from -0.125 to 0.125
- enc_stream: bfloat16 [16384, 1536], P('dp'), may hold values from -6 to 6
- enc_attn: bfloat16 [16384, 1536], P('dp', 'tensor'), may hold values from -6 to 6
- enc_proj: bfloat16 [1536, 1536], P('tensor'), may hold values from -0.15625 to 0.15625
- layer_scale: float32 [1536], replicated, may hold values from 0.1 to 1
- enc_gain: float32 [1536], replicated, may hold values from 0.25 to 1.75
- enc_bias: float32 [1536], replicated, may hold values from -2.5 to 2.5
- patch_index: int32 [16384], P('dp'), may hold values from 0 to 255, as said below
Outputs:
- grad_hidden: bfloat16 [16384, 3072], P('dp', 'tensor')
- grad_branch: bfloat16 [16384, 3072], P('dp', 'tensor')
- grad_w_gate: float32 [3072, 3072], P('dp', 'tensor')
- grad_w_in: float32 [3072, 2048], P('dp', 'tensor')
- grad_w_mid: float32 [2048, 2048], P('tensor', 'dp')
- grad_w_out: float32 [2048, 1536], P('dp', 'tensor')
The draws below stay inside these ranges and needn't reach their ends.
Inputs may be any that keep to these rules, and one draw needn't show every extreme that they name: `patch_index`: each aligned block of 256 entries is a permutation of 0 to 255.
All inputs are finite; a program needn't handle non-finite values.
Results may differ from the reference program's by a relative error of at most 0.0095.
Values may be sent and summed in bfloat16 or wider, within the bound.
No kernel may reach another device: no remote copies, remote signals or barrier semaphores. Data moves between devices by JAX's collectives and lax.ppermute only.
A program may use at most 128 MiB of HBM per device.

```python
import math
import jax
import jax.numpy as jnp
from jax import lax

D = 3072
H = 2048
E = 1536
FREQ = 256
TOK_DEV = 256
TOKENS = 16384
IMAGES = 4
N_DP = 64


def draw_patch_index(key, part):
    key = jax.random.fold_in(key, 7)
    block_count = TOKENS // TOK_DEV
    block_keys = jax.random.split(key, block_count)
    orders = jax.vmap(lambda block_key: jax.random.permutation(block_key, TOK_DEV))(block_keys)
    return orders.reshape(-1).astype(jnp.int32)


def with_ends(values, key, least, largest):
    index_at = [jax.random.randint(jax.random.fold_in(key, axis), (), 0, length) for axis, length in enumerate(values.shape)]
    widest = values.shape.index(max(values.shape))
    beside = index_at[:widest] + [(index_at[widest] + 1) % values.shape[widest]] + index_at[widest + 1:]
    return values.at[tuple(index_at)].set(least).at[tuple(beside)].set(largest)


def level_of(rng, dims, shards, smallest, high):
    gain = 1.0
    for axis_at, parts in shards:
        heights = jax.random.uniform(jax.random.fold_in(jax.random.fold_in(rng, 6), axis_at), (parts,), jnp.float32, smallest / len(shards), high / len(shards))
        gain = gain * jnp.repeat(jnp.exp(heights), dims[axis_at] // parts).reshape((-1,) + (1,) * (len(dims) - 1 - axis_at))
    return gain


def normal_values(stream_key, extent, spread, reach, cuts=(), held_as=jnp.bfloat16):
    level = level_of(stream_key, extent, cuts, -0.22, 0.18) if cuts else 1.0
    array = jax.random.normal(stream_key, extent, jnp.float32) * spread * level
    return jnp.minimum(jnp.maximum(array, -reach), reach).astype(held_as)


def setup_inputs(seed: int = 0) -> dict:
    keys = jax.random.split(jax.random.key(seed), 17)
    hidden = normal_values(keys[0], (TOKENS, D), 1.0, 6.0, ((0, 64),))
    branch = normal_values(keys[1], (TOKENS, D), 1.0, 6.0, ((0, 64),))
    up_grad = normal_values(keys[2], (TOKENS, D), 1.0, 6.0, ((0, 64), (1, 4)))
    timesteps = with_ends(jax.random.randint(keys[3], (IMAGES,), 0, 1000), jax.random.fold_in(keys[3], 1), 0, 999).astype(jnp.int32)
    w_time = normal_values(keys[4], (FREQ, D), FREQ ** -0.5, 0.375)
    w_gate = normal_values(keys[5], (D, D), D ** -0.5, 0.109375, ((0, 64), (1, 4)))
    w_in = normal_values(keys[6], (D, H), D ** -0.5, 0.109375, ((0, 64), (1, 4)))
    w_mid = normal_values(keys[7], (H, H), H ** -0.5, 0.125, ((0, 4), (1, 64)))
    w_out = normal_values(keys[8], (H, E), H ** -0.5, 0.125, ((0, 64), (1, 4)))
    enc_stream = normal_values(keys[9], (TOKENS, E), 1.0, 6.0, ((0, 64),))
    enc_attn = normal_values(keys[10], (TOKENS, E), 1.0, 6.0, ((0, 64), (1, 4)))
    enc_proj = normal_values(keys[11], (E, E), E ** -0.5, 0.15625, ((0, 4),))
    layer_scale = jnp.clip(jnp.exp(jax.random.uniform(keys[12], (E,), jnp.float32, math.log(0.1), math.log(1.0))), 0.1, 1.0)
    enc_gain = jnp.clip(1.0 + 0.15 * jax.random.normal(keys[13], (E,), jnp.float32), 0.25, 1.75)
    enc_bias = normal_values(keys[14], (E,), 0.4, 2.5, (), jnp.float32)
    patch_index = draw_patch_index(jax.random.fold_in(keys[16], 71), 0)
    return dict(hidden=hidden, branch=branch, up_grad=up_grad, timesteps=timesteps, w_time=w_time, w_gate=w_gate, w_in=w_in, w_mid=w_mid, w_out=w_out, enc_stream=enc_stream, enc_attn=enc_attn, enc_proj=enc_proj, layer_scale=layer_scale, enc_gain=enc_gain, enc_bias=enc_bias, patch_index=patch_index)


eps_norm = 1e-06
loss_scale = 1024.0

def silu_slope(values):
    sigmoid_part = jax.nn.sigmoid(values)
    return sigmoid_part * (1.0 + values * (1.0 - sigmoid_part))

def time_features(timesteps):
    half_freq = FREQ // 2
    frequency = jnp.exp(-math.log(10000.0) * jnp.arange(half_freq, dtype=jnp.float32) / half_freq)
    angles = timesteps.astype(jnp.float32)[:, None] * frequency[None, :]
    return jnp.concatenate([jnp.cos(angles), jnp.sin(angles)], axis=1).astype(jnp.bfloat16)

def encoder_features(enc_stream, enc_attn, enc_proj, layer_scale, enc_gain, enc_bias):
    projected = jnp.dot(enc_attn, enc_proj, preferred_element_type=jnp.float32)
    stream = enc_stream.astype(jnp.float32) + layer_scale * projected
    centre = lax.optimization_barrier(jnp.mean(stream, axis=1, keepdims=True))
    centred = stream - centre
    variance = lax.optimization_barrier(jnp.mean(centred * centred, axis=1, keepdims=True))
    normed = centred * lax.rsqrt(variance + eps_norm) * enc_gain + enc_bias
    length = lax.optimization_barrier(jnp.sum(normed * normed, axis=1, keepdims=True))
    return (normed * lax.rsqrt(length + eps_norm)).astype(jnp.bfloat16)

def reference(hidden, branch, up_grad, timesteps, w_time, w_gate, w_in, w_mid, w_out, enc_stream, enc_attn, enc_proj, layer_scale, enc_gain, enc_bias, patch_index):
    features = encoder_features(enc_stream, enc_attn, enc_proj, layer_scale, enc_gain, enc_bias)
    token_ids = jnp.arange(TOKENS, dtype=jnp.int32)
    piece_rows = TOK_DEV // N_DP
    target_dev = token_ids // TOK_DEV
    source_row = patch_index // piece_rows * TOK_DEV + target_dev * piece_rows + patch_index % piece_rows
    aligned = jnp.take(features, source_row.astype(jnp.int32), axis=0).astype(jnp.float32)
    image_count = timesteps.shape[0]
    image_rows = TOKENS // image_count
    t_freq = time_features(timesteps)
    steps_emb = jax.nn.silu(jnp.dot(t_freq, w_time, preferred_element_type=jnp.float32)).astype(jnp.bfloat16)
    gate = jnp.dot(steps_emb, w_gate, preferred_element_type=jnp.float32)
    hidden_img = hidden.astype(jnp.float32).reshape(image_count, image_rows, D)
    branch_img = branch.astype(jnp.float32).reshape(image_count, image_rows, D)
    block_out = (hidden_img + gate[:, None, :] * branch_img).reshape(TOKENS, D).astype(jnp.bfloat16)
    pre_one = jnp.dot(block_out, w_in, preferred_element_type=jnp.float32)
    act_one = jax.nn.silu(pre_one).astype(jnp.bfloat16)
    pre_two = jnp.dot(act_one, w_mid, preferred_element_type=jnp.float32)
    act_two = jax.nn.silu(pre_two).astype(jnp.bfloat16)
    proj_out = jnp.dot(act_two, w_out, preferred_element_type=jnp.float32)
    square_sum = lax.optimization_barrier(jnp.sum(proj_out * proj_out, axis=1, keepdims=True))
    inner_sum = lax.optimization_barrier(jnp.sum(proj_out * aligned, axis=1, keepdims=True))
    inv_len = lax.rsqrt(square_sum + eps_norm)
    d_out = (-loss_scale * (aligned * inv_len - inner_sum * inv_len * inv_len * inv_len * proj_out)).astype(jnp.bfloat16)
    grad_w_out = jnp.dot(act_two.T, d_out, preferred_element_type=jnp.float32)
    d_two = (jnp.dot(d_out, w_out.T, preferred_element_type=jnp.float32) * silu_slope(pre_two)).astype(jnp.bfloat16)
    grad_w_mid = jnp.dot(act_one.T, d_two, preferred_element_type=jnp.float32)
    d_one = (jnp.dot(d_two, w_mid.T, preferred_element_type=jnp.float32) * silu_slope(pre_one)).astype(jnp.bfloat16)
    grad_w_in = jnp.dot(block_out.T, d_one, preferred_element_type=jnp.float32)
    total_grad = up_grad.astype(jnp.float32) + jnp.dot(d_one, w_in.T, preferred_element_type=jnp.float32)
    grad_hidden = total_grad.astype(jnp.bfloat16)
    total_img = total_grad.reshape(image_count, image_rows, D)
    grad_branch = (gate[:, None, :] * total_img).reshape(TOKENS, D).astype(jnp.bfloat16)
    per_image = lax.optimization_barrier(jnp.sum(total_img * branch_img, axis=1))
    grad_w_gate = jnp.dot(steps_emb.astype(jnp.float32).T, per_image, precision=lax.Precision.HIGHEST)
    return (grad_hidden, grad_branch, grad_w_gate, grad_w_in, grad_w_mid, grad_w_out)
```

```python
import math

import jax
import jax.numpy as jnp
from jax import lax
from jax.sharding import Mesh
from jax.sharding import PartitionSpec as P

FREQ = 256
SEQ = 4096
DP = ("xl", "z", "y")
TENSOR = ("xh", "core")

eps_norm = 1e-06
loss_scale = 1024.0
bf16 = jnp.bfloat16
f32 = jnp.float32


def silu_slope(values):
    sigmoid_part = jax.nn.sigmoid(values)
    return sigmoid_part * (1.0 + values * (1.0 - sigmoid_part))


def time_features(timesteps):
    half_freq = FREQ // 2
    frequency = jnp.exp(-math.log(10000.0) * jnp.arange(half_freq, dtype=jnp.float32) / half_freq)
    angles = timesteps.astype(jnp.float32)[:, None] * frequency[None, :]
    return jnp.concatenate([jnp.cos(angles), jnp.sin(angles)], axis=1).astype(jnp.bfloat16)


def contract_rows(left, right):
    return lax.dot_general(
        left, right, (((0,), (0,)), ((), ())), preferred_element_type=jnp.float32
    )


def contract_cols(left, right):
    return lax.dot_general(
        left, right, (((1,), (1,)), ((), ())), preferred_element_type=jnp.float32
    )


def swap(value, axis):
    return lax.ppermute(value, axis, [(0, 1), (1, 0)])


def shift(value, axis, step):
    count = lax.axis_size(axis)
    return lax.ppermute(value, axis, [(i, (i + step) % count) for i in range(count)])


def in_order(own, other, axis):
    first = lax.axis_index(axis) == 0
    return jnp.stack([jnp.where(first, own, other), jnp.where(first, other, own)])


def pick(values, index, axis=0):
    return lax.dynamic_index_in_dim(values, index, axis, keepdims=False)


def gather_weight(part):
    rows, cols = part.shape
    by_z = lax.all_gather(part, "z", axis=0)
    near, far = by_z[:4], by_z[4:]
    near = in_order(near, swap(near, "xl"), "xl")
    near = lax.all_gather(near, "y", axis=0)
    far = lax.all_gather(far, "y", axis=0)
    far = in_order(far, swap(far, "xl"), "xl")
    whole = jnp.concatenate(
        [near.transpose(1, 2, 0, 3, 4), far.transpose(0, 2, 1, 3, 4)], axis=1
    )
    return whole.reshape(64 * rows, cols)


def sum_over_y(parts, axis):
    here = lax.axis_index("y")
    total = pick(parts, here, axis).astype(f32)
    for step in (1, 2, 3):
        sent = pick(parts, (here + step) % 4, axis)
        total = total + shift(sent, "y", step).astype(f32)
    return total


def sum_over_x(parts):
    here = lax.axis_index("xl")
    got = swap(pick(parts, 1 - here), "xl")
    return pick(parts, here).astype(f32) + got.astype(f32)


def scatter_weight(grad):
    total_rows, cols = grad.shape
    rows = total_rows // 64
    parts = grad.astype(bf16).reshape(2, 8, 4, rows, cols)
    near = sum_over_x(sum_over_y(parts[:, :4], 2).astype(bf16))
    far = sum_over_y(sum_over_x(parts[:, 4:]).astype(bf16), 1)
    both = jnp.concatenate([near, far], axis=0).astype(bf16)
    got = lax.all_to_all(both, "z", 0, 0, tiled=True)
    return jnp.sum(got.astype(f32), axis=0)


def tensor_scatter(partial):
    width = partial.shape[1] // 4
    core = lax.axis_index("core")
    high = lax.axis_index("xh")

    def block(xh, c):
        return lax.dynamic_slice_in_dim(partial, (2 * xh + c) * width, width, 1)

    got = swap(
        jnp.stack([block(1 - high, 1 - core), block(high, 1 - core)]).astype(bf16), "core"
    ).astype(f32)
    away = block(1 - high, core).astype(f32) + got[0]
    own = block(high, core).astype(f32) + got[1]
    return own + swap(away.astype(bf16), "xh").astype(f32)


def tensor_gather(part):
    pair = in_order(part, swap(part, "xh"), "xh")
    quad = in_order(pair, swap(pair, "core"), "core")
    return jnp.concatenate([quad[0, 0], quad[1, 0], quad[0, 1], quad[1, 1]], axis=1)


def spread(row, axes, count):
    return lax.all_to_all(
        jnp.broadcast_to(row[None], (count,) + row.shape), axes, 0, 0, tiled=True
    )


def body(
    hidden,
    branch,
    up_grad,
    timesteps,
    w_time,
    w_gate,
    w_in,
    w_mid,
    w_out,
    enc_stream,
    enc_attn,
    enc_proj,
    layer_scale,
    enc_gain,
    enc_bias,
    patch_index,
):
    tensor_index = lax.axis_index(TENSOR)
    data_index = lax.axis_index(DP)
    token_rows = hidden.shape[0]
    image_count = timesteps.shape[0]
    image_index = data_index * token_rows // SEQ

    t_freq = time_features(timesteps)
    steps_all = jax.nn.silu(jnp.dot(t_freq, w_time, preferred_element_type=jnp.float32)).astype(
        jnp.bfloat16
    )
    gate_share_rows = w_gate.shape[0]
    own_emb_cols = lax.dynamic_slice_in_dim(
        steps_all, data_index * gate_share_rows, gate_share_rows, 1
    )
    gate_partial = jnp.dot(own_emb_cols, w_gate, preferred_element_type=jnp.float32)
    gate_sent = jnp.repeat(gate_partial, 64 // image_count, axis=0)
    gate_cols = jnp.sum(
        lax.all_to_all(gate_sent, DP, 0, 0, tiled=True), axis=0, keepdims=True
    )
    gate_all = lax.all_gather(gate_cols, TENSOR, axis=1, tiled=True)

    in_table = gather_weight(w_in)
    mid_turned = gather_weight(w_mid.T)
    out_table = gather_weight(w_out)

    enc_width = enc_stream.shape[1]
    enc_share = enc_width // 4
    enc_start = tensor_index * enc_share
    enc_partial = jnp.dot(enc_attn, enc_proj, preferred_element_type=jnp.float32)
    projected = tensor_scatter(enc_partial)

    def own_cols(values):
        return lax.dynamic_slice_in_dim(values, enc_start, enc_share, values.ndim - 1)

    gain, bias = own_cols(enc_gain), own_cols(enc_bias)
    stream = own_cols(enc_stream).astype(f32) + own_cols(layer_scale) * projected
    local_mean = jnp.mean(stream, axis=1)
    local = stream - local_mean[:, None]
    gained = gain * local
    moments = jnp.stack(
        [
            local_mean,
            jnp.sum(local * local, axis=1),
            jnp.sum(gained * gained, axis=1),
            jnp.sum(gained * gain, axis=1),
            jnp.sum(gained * bias, axis=1),
            jnp.full_like(local_mean, jnp.sum(gain * gain)),
            jnp.full_like(local_mean, jnp.sum(gain * bias)),
            jnp.full_like(local_mean, jnp.sum(bias * bias)),
        ]
    )
    shared = spread(moments, TENSOR, 4)
    means = shared[:, 0]
    centre = jnp.mean(means, axis=0)
    offs = means - centre
    variance = (jnp.sum(shared[:, 1], axis=0) + enc_share * jnp.sum(offs * offs, axis=0)) / enc_width
    rstd = lax.rsqrt(variance + eps_norm)
    quad = jnp.sum(shared[:, 2] + offs * (2.0 * shared[:, 3] + offs * shared[:, 5]), axis=0)
    cross = jnp.sum(shared[:, 4] + offs * shared[:, 6], axis=0)
    length = rstd * (rstd * quad + 2.0 * cross) + jnp.sum(shared[:, 7], axis=0)
    normed = (stream - centre[:, None]) * rstd[:, None] * gain + bias
    own_unit = (normed * lax.rsqrt(jnp.maximum(length, 0.0) + eps_norm)[:, None]).astype(bf16)
    received = lax.all_to_all(own_unit, DP, split_axis=0, concat_axis=0, tiled=True)
    aligned = jnp.take(received, patch_index, axis=0).astype(jnp.float32)

    block_out = (hidden.astype(jnp.float32) + gate_all * branch.astype(jnp.float32)).astype(
        jnp.bfloat16
    )
    pre_one = jnp.dot(block_out, in_table, preferred_element_type=jnp.float32)
    act_one = jax.nn.silu(pre_one).astype(jnp.bfloat16)
    pre_two = tensor_scatter(contract_cols(act_one, mid_turned))
    act_two = tensor_gather(jax.nn.silu(pre_two).astype(jnp.bfloat16))
    proj_out = jnp.dot(act_two, out_table, preferred_element_type=jnp.float32)
    square_sum, inner_sum = lax.psum(
        (jnp.sum(proj_out * proj_out, axis=1), jnp.sum(proj_out * aligned, axis=1)), TENSOR
    )
    inv_len = lax.rsqrt(square_sum + eps_norm)[:, None]
    inner_col = inner_sum[:, None]
    d_out = (
        -loss_scale * (aligned * inv_len - inner_col * inv_len * inv_len * inv_len * proj_out)
    ).astype(jnp.bfloat16)

    back = tensor_scatter(contract_cols(d_out, out_table))
    d_two = tensor_gather((back * silu_slope(pre_two)).astype(jnp.bfloat16))
    grad_w_out = scatter_weight(contract_rows(act_two, d_out))
    d_one = (
        jnp.dot(d_two, mid_turned, preferred_element_type=jnp.float32) * silu_slope(pre_one)
    ).astype(jnp.bfloat16)
    grad_w_mid = scatter_weight(contract_rows(d_two, act_one)).T
    stream_share = tensor_scatter(contract_cols(d_one, in_table))
    grad_w_in = scatter_weight(contract_rows(block_out, d_one))
    total_grad = up_grad.astype(jnp.float32) + stream_share
    grad_hidden = total_grad.astype(jnp.bfloat16)
    grad_branch = (gate_cols * total_grad).astype(jnp.bfloat16)
    model_share = w_gate.shape[1]
    branch_cols = lax.dynamic_slice_in_dim(
        branch, tensor_index * model_share, model_share, 1
    ).astype(jnp.float32)
    device_sum = jnp.sum(total_grad * branch_cols, axis=0)
    all_sums = spread(device_sum, DP, 64)
    image_sums = jnp.sum(all_sums.reshape(image_count, 64 // image_count, model_share), axis=1)
    grad_w_gate = lax.dot_general(
        own_emb_cols.astype(jnp.float32),
        image_sums,
        (((0,), (0,)), ((), ())),
        precision=lax.Precision.HIGHEST,
        preferred_element_type=jnp.float32,
    )
    return (grad_hidden, grad_branch, grad_w_gate, grad_w_in, grad_w_mid, grad_w_out)


def solution(mesh):
    split = Mesh(mesh.devices.reshape(2, 8, 4, 2, 2), DP + TENSOR)
    return jax.shard_map(
        body,
        mesh=split,
        in_specs=(
            P(DP, None),
            P(DP, None),
            P(DP, TENSOR),
            P(),
            P(),
            P(DP, TENSOR),
            P(DP, TENSOR),
            P(TENSOR, DP),
            P(DP, TENSOR),
            P(DP, None),
            P(DP, TENSOR),
            P(TENSOR, None),
            P(),
            P(),
            P(),
            P(DP),
        ),
        out_specs=(
            P(DP, TENSOR),
            P(DP, TENSOR),
            P(DP, TENSOR),
            P(DP, TENSOR),
            P(TENSOR, DP),
            P(DP, TENSOR),
        ),
        check_vma=False,
    )
```

```python
import math

import jax
import jax.numpy as jnp
from jax import lax
from jax.sharding import Mesh
from jax.sharding import PartitionSpec as P

FREQ = 256
SEQ = 4096
DP = ("xl", "z", "y")
TENSOR = ("xh", "core")

eps_norm = 1e-06
loss_scale = 1024.0
bf16 = jnp.bfloat16
f32 = jnp.float32


def silu_slope(values):
    sigmoid_part = jax.nn.sigmoid(values)
    return sigmoid_part * (1.0 + values * (1.0 - sigmoid_part))


def time_features(timesteps):
    half_freq = FREQ // 2
    frequency = jnp.exp(-math.log(10000.0) * jnp.arange(half_freq, dtype=jnp.float32) / half_freq)
    angles = timesteps.astype(jnp.float32)[:, None] * frequency[None, :]
    return jnp.concatenate([jnp.cos(angles), jnp.sin(angles)], axis=1).astype(jnp.bfloat16)


def contract_rows(left, right):
    return lax.dot_general(
        left, right, (((0,), (0,)), ((), ())), preferred_element_type=jnp.float32
    )


def contract_cols(left, right):
    return lax.dot_general(
        left, right, (((1,), (1,)), ((), ())), preferred_element_type=jnp.float32
    )


def peer(value, axis, bits):
    count = lax.axis_size(axis)
    return lax.ppermute(value, axis, [(i, i ^ bits) for i in range(count)])


def peers(value, axis):
    return [peer(value, axis, bits) for bits in (1, 2, 3)]


def after(value, *earlier):
    return lax.optimization_barrier((value,) + earlier)[0]


def pick(values, index, axis=0):
    return lax.dynamic_index_in_dim(values, index, axis, keepdims=False)


def pair_in_order(own, other, first):
    return [jnp.where(first, own, other), jnp.where(first, other, own)]


def quad_in_order(blocks, index):
    near = pair_in_order(blocks[0], blocks[1], index % 2 == 0)
    far = pair_in_order(blocks[2], blocks[3], index % 2 == 0)
    low_first = index < 2
    return [jnp.where(low_first, a, b) for a, b in zip(near, far)] + [
        jnp.where(low_first, b, a) for a, b in zip(near, far)
    ]


def spread(block, axes):
    count = lax.axis_size(axes)
    return lax.all_to_all(
        jnp.broadcast_to(block[None], (count,) + block.shape), axes, 0, 0, tiled=True
    )


def exchange_sum(parts, axes):
    got = lax.all_to_all(parts.astype(bf16), axes, 0, 0, tiled=True)
    return jnp.sum(got.astype(f32), axis=0)


def gather_rest(by_z):
    rows, cols = by_z.shape[1:]
    whole = spread(by_z, ("xl", "y")).reshape(2, 4, 8, rows, cols)
    return whole.transpose(0, 2, 1, 3, 4).reshape(64 * rows, cols)


def gather_xy(part):
    pair = jnp.stack(pair_in_order(part, peer(part, "xl", 1), lax.axis_index("xl") == 0))
    quad = quad_in_order([pair] + peers(pair, "y"), lax.axis_index("y"))
    return jnp.stack(quad, axis=1)


def gather_z(part, cols):
    rows = part.shape[2]
    whole = lax.all_gather(part, "z", axis=0)[..., :cols]
    return whole.transpose(1, 0, 2, 3, 4).reshape(64 * rows, cols)


def xy_parts(grad):
    total_rows, cols = grad.shape
    rows = total_rows // 64
    parts = grad.reshape(2, 8, 4, rows, cols).transpose(0, 2, 1, 3, 4)
    return parts.reshape(8, 8, rows, cols)


def scatter_z_first(grad):
    total_rows, cols = grad.shape
    rows = total_rows // 64
    parts = grad.reshape(2, 8, 4, rows, cols).transpose(1, 0, 2, 3, 4)
    by_z = lax.psum_scatter(
        parts.reshape(8, 8 * rows, cols), "z", scatter_dimension=0, tiled=False
    ).reshape(2, 4, rows, cols)
    x_here, y_here = lax.axis_index("xl"), lax.axis_index("y")
    by_x = (
        pick(by_z, x_here).astype(f32) + peer(pick(by_z, 1 - x_here), "xl", 1).astype(f32)
    ).astype(bf16)
    total = pick(by_x, y_here).astype(f32)
    for bits in (1, 2, 3):
        total = total + peer(pick(by_x, y_here ^ bits), "y", bits).astype(f32)
    return total


def tensor_scatter(product):
    core = lax.axis_index("core")
    high = lax.axis_index("xh")

    def block(xh, c):
        return product(2 * xh + c)

    far_got = peer(block(1 - high, 1 - core).astype(bf16), "core", 1)
    own_got = peer(block(high, 1 - core).astype(bf16), "core", 1)
    away = block(1 - high, core) + far_got.astype(f32)
    away = away.astype(bf16)
    away_got = peer(away, "xh", 1)
    return block(high, core) + own_got.astype(f32) + away_got.astype(f32), away


def row_block(table, index):
    width = table.shape[0] // 4
    return lax.dynamic_slice_in_dim(table, index * width, width, 0)


def tensor_blocks(part):
    beside = peer(part, "core", 1)
    across = peer(part, "xh", 1)
    corner = peer(across, "core", 1)
    return quad_in_order([part, beside, across, corner], lax.axis_index(TENSOR))


def tensor_gather(part):
    return jnp.concatenate(tensor_blocks(part), axis=1)


def body(
    hidden,
    branch,
    up_grad,
    timesteps,
    w_time,
    w_gate,
    w_in,
    w_mid,
    w_out,
    enc_stream,
    enc_attn,
    enc_proj,
    layer_scale,
    enc_gain,
    enc_bias,
    patch_index,
):
    tensor_index = lax.axis_index(TENSOR)
    data_index = lax.axis_index(DP)
    token_rows = hidden.shape[0]
    image_count = timesteps.shape[0]
    image_index = data_index * token_rows // SEQ

    t_freq = time_features(timesteps)
    steps_all = jax.nn.silu(jnp.dot(t_freq, w_time, preferred_element_type=jnp.float32)).astype(
        jnp.bfloat16
    )
    gate_share_rows = w_gate.shape[0]
    own_emb_cols = lax.dynamic_slice_in_dim(
        steps_all, data_index * gate_share_rows, gate_share_rows, 1
    )
    gate_partial = jnp.dot(own_emb_cols, w_gate, preferred_element_type=jnp.float32)
    model_share = w_gate.shape[1]
    x_here, z_here = lax.axis_index("xl"), lax.axis_index("z")
    z_high = z_here // 4
    by_image = gate_partial.reshape(2, 2, model_share)
    by_z = pick(by_image, z_high, 1) + peer(pick(by_image, 1 - z_high, 1), "z", 4)
    by_z = by_z + sum(peers(by_z, "z"))
    to_rest = jnp.broadcast_to(by_z[:, None], (2, 16, model_share)).reshape(32, model_share)
    from_rest = lax.all_to_all(to_rest, ("xl", "y") + TENSOR, 0, 0, tiled=True)
    gate_all = jnp.sum(from_rest.reshape(8, 4 * model_share), axis=0, keepdims=True)
    enc_width = enc_stream.shape[1]
    enc_share = enc_width // 4
    enc_start = tensor_index * enc_share
    projected, _ = tensor_scatter(
        lambda t: jnp.dot(
            enc_attn,
            lax.dynamic_slice_in_dim(enc_proj, t * enc_share, enc_share, 1),
            preferred_element_type=jnp.float32,
        )
    )

    in_by_z = spread(w_in, "z")
    hidden_share, out_share = w_in.shape[1], w_out.shape[1]
    both_tables = gather_xy(
        jnp.pad(jnp.concatenate([w_mid.T, w_out], axis=1), ((0, 0), (0, hidden_share - out_share)))
    )
    both_tables = after(both_tables, in_by_z)
    in_by_z, projected, gate_all = lax.optimization_barrier((in_by_z, projected, gate_all))
    gate_cols = lax.dynamic_slice_in_dim(gate_all, tensor_index * model_share, model_share, 1)
    in_table = gather_rest(in_by_z)
    mid_turned = gather_z(both_tables[..., :hidden_share], hidden_share)
    out_table = gather_z(both_tables[..., hidden_share:], out_share)

    def own_cols(values):
        return lax.dynamic_slice_in_dim(values, enc_start, enc_share, values.ndim - 1)

    gain, bias = own_cols(enc_gain), own_cols(enc_bias)
    stream = own_cols(enc_stream).astype(f32) + own_cols(layer_scale) * projected
    local_mean = jnp.mean(stream, axis=1)
    local = stream - local_mean[:, None]
    gained = gain * local
    moments = jnp.stack(
        [
            local_mean,
            jnp.sum(local * local, axis=1),
            jnp.sum(gained * gained, axis=1),
            jnp.sum(gained * gain, axis=1),
            jnp.sum(gained * bias, axis=1),
        ]
    )
    block_out = (hidden.astype(jnp.float32) + gate_all * branch.astype(jnp.float32)).astype(
        jnp.bfloat16
    )
    pre_one = jnp.dot(block_out, in_table, preferred_element_type=jnp.float32)
    act_one = jax.nn.silu(pre_one).astype(jnp.bfloat16)
    shared = after(jnp.stack([moments] + peers(moments, TENSOR)), act_one)
    sharer = tensor_index ^ jnp.arange(4, dtype=jnp.int32)

    def share_sums(values):
        return jnp.take(jnp.sum(values.reshape(4, enc_share), axis=1), sharer)[:, None]

    means = shared[:, 0]
    centre = jnp.mean(means, axis=0)
    offs = means - centre
    variance = (jnp.sum(shared[:, 1], axis=0) + enc_share * jnp.sum(offs * offs, axis=0)) / enc_width
    rstd = lax.rsqrt(variance + eps_norm)
    quad = jnp.sum(
        shared[:, 2] + offs * (2.0 * shared[:, 3] + offs * share_sums(enc_gain * enc_gain)), axis=0
    )
    cross = jnp.sum(shared[:, 4] + offs * share_sums(enc_gain * enc_bias), axis=0)
    length = rstd * (rstd * quad + 2.0 * cross) + jnp.sum(enc_bias * enc_bias)
    normed = (stream - centre[:, None]) * rstd[:, None] * gain + bias
    own_unit = (normed * lax.rsqrt(jnp.maximum(length, 0.0) + eps_norm)[:, None]).astype(bf16)
    pre_two, _ = tensor_scatter(
        lambda t: contract_cols(act_one, row_block(mid_turned, t))
    )
    received = lax.all_to_all(own_unit, DP, split_axis=0, concat_axis=0, tiled=True)
    aligned = jnp.take(received, patch_index, axis=0).astype(jnp.float32)
    act_two = tensor_gather(jax.nn.silu(pre_two).astype(jnp.bfloat16))
    proj_out = jnp.dot(act_two, out_table, preferred_element_type=jnp.float32)
    square_sum, inner_sum = lax.psum(
        (jnp.sum(proj_out * proj_out, axis=1), jnp.sum(proj_out * aligned, axis=1)), TENSOR
    )
    inv_len = lax.rsqrt(square_sum + eps_norm)[:, None]
    inner_col = inner_sum[:, None]
    d_out = (
        -loss_scale * (aligned * inv_len - inner_col * inv_len * inv_len * inv_len * proj_out)
    ).astype(jnp.bfloat16)

    back, _ = tensor_scatter(lambda t: contract_cols(d_out, row_block(out_table, t)))
    d_two = tensor_gather((back * silu_slope(pre_two)).astype(jnp.bfloat16))
    grad_w_out = scatter_z_first(contract_rows(act_two, d_out).astype(bf16))
    d_one = (
        jnp.dot(d_two, mid_turned, preferred_element_type=jnp.float32) * silu_slope(pre_one)
    ).astype(jnp.bfloat16)
    grad_w_mid = scatter_z_first(contract_rows(d_two, act_one).astype(bf16)).T
    grad_in = contract_rows(block_out, d_one).astype(bf16)
    stream_share, _ = tensor_scatter(
        lambda t: contract_cols(d_one, row_block(in_table, t))
    )
    in_by_xy = exchange_sum(xy_parts(grad_in), ("xl", "y")).astype(bf16)
    stream_share = after(stream_share, in_by_xy)
    grad_w_in = exchange_sum(in_by_xy, "z")
    total_grad = up_grad.astype(jnp.float32) + stream_share
    grad_hidden = total_grad.astype(jnp.bfloat16)
    grad_branch = (gate_cols * total_grad).astype(jnp.bfloat16)
    branch_cols = lax.dynamic_slice_in_dim(
        branch, tensor_index * model_share, model_share, 1
    ).astype(jnp.float32)
    image_sum = jnp.sum(total_grad * branch_cols, axis=0, keepdims=True)
    image_sum = image_sum + sum(peers(image_sum, "y"))
    image_sum = image_sum + sum(peers(image_sum, "z"))
    z_pair = jnp.concatenate(
        pair_in_order(image_sum, peer(image_sum, "z", 4), z_high == 0), axis=0
    )
    image_sums = jnp.concatenate(
        pair_in_order(z_pair, peer(z_pair, "xl", 1), x_here == 0), axis=0
    )
    grad_w_gate = lax.dot_general(
        own_emb_cols.astype(jnp.float32),
        image_sums,
        (((0,), (0,)), ((), ())),
        precision=lax.Precision.HIGHEST,
        preferred_element_type=jnp.float32,
    )
    return (grad_hidden, grad_branch, grad_w_gate, grad_w_in, grad_w_mid, grad_w_out)


def solution(mesh):
    split = Mesh(mesh.devices.reshape(2, 8, 4, 2, 2), DP + TENSOR)
    return jax.shard_map(
        body,
        mesh=split,
        in_specs=(
            P(DP, None),
            P(DP, None),
            P(DP, TENSOR),
            P(),
            P(),
            P(DP, TENSOR),
            P(DP, TENSOR),
            P(TENSOR, DP),
            P(DP, TENSOR),
            P(DP, None),
            P(DP, TENSOR),
            P(TENSOR, None),
            P(),
            P(),
            P(),
            P(DP),
        ),
        out_specs=(
            P(DP, TENSOR),
            P(DP, TENSOR),
            P(DP, TENSOR),
            P(DP, TENSOR),
            P(TENSOR, DP),
            P(DP, TENSOR),
        ),
        check_vma=False,
    )
```

```python
import math

import jax
import jax.numpy as jnp
from jax import lax
from jax.sharding import Mesh
from jax.sharding import PartitionSpec as P

FREQ = 256
SEQ = 4096
DP = ("xl", "z", "y")
TENSOR = ("xh", "core")

eps_norm = 1e-06
loss_scale = 1024.0
bf16 = jnp.bfloat16
f32 = jnp.float32


def silu_slope(values):
    sigmoid_part = jax.nn.sigmoid(values)
    return sigmoid_part * (1.0 + values * (1.0 - sigmoid_part))


def time_features(timesteps):
    half_freq = FREQ // 2
    frequency = jnp.exp(-math.log(10000.0) * jnp.arange(half_freq, dtype=jnp.float32) / half_freq)
    angles = timesteps.astype(jnp.float32)[:, None] * frequency[None, :]
    return jnp.concatenate([jnp.cos(angles), jnp.sin(angles)], axis=1).astype(jnp.bfloat16)


def contract_rows(left, right):
    return lax.dot_general(
        left, right, (((0,), (0,)), ((), ())), preferred_element_type=jnp.float32
    )


def contract_cols(left, right):
    return lax.dot_general(
        left, right, (((1,), (1,)), ((), ())), preferred_element_type=jnp.float32
    )


def peer(value, axis, bits):
    count = lax.axis_size(axis)
    return lax.ppermute(value, axis, [(i, i ^ bits) for i in range(count)])


def peers(value, axis):
    return [peer(value, axis, bits) for bits in (1, 2, 3)]


def after(value, *earlier):
    return lax.optimization_barrier((value,) + earlier)[0]


def pick(values, index, axis=0):
    return lax.dynamic_index_in_dim(values, index, axis, keepdims=False)


def pair_in_order(own, other, first):
    return [jnp.where(first, own, other), jnp.where(first, other, own)]


def quad_in_order(blocks, index):
    near = pair_in_order(blocks[0], blocks[1], index % 2 == 0)
    far = pair_in_order(blocks[2], blocks[3], index % 2 == 0)
    low_first = index < 2
    return [jnp.where(low_first, a, b) for a, b in zip(near, far)] + [
        jnp.where(low_first, b, a) for a, b in zip(near, far)
    ]


def halves(value):
    high = lax.reduce_precision(value, 8, 7)
    return jnp.stack([high.astype(bf16), (value - high).astype(bf16)])


def pad_to(value, shape):
    return jnp.pad(value, [(0, full - own) for own, full in zip(value.shape, shape)])


def exchange(parts, axes):
    return lax.all_to_all(parts, axes, 0, 0, tiled=True)


def exchange_sum(parts, axes):
    got = lax.all_to_all(parts.astype(bf16), axes, 0, 0, tiled=True)
    return jnp.sum(got.astype(f32), axis=0)


def gather_xy(part):
    pair = jnp.stack(pair_in_order(part, peer(part, "xl", 1), lax.axis_index("xl") == 0))
    quad = quad_in_order([pair] + peers(pair, "y"), lax.axis_index("y"))
    return jnp.stack(quad, axis=1)


def gather_z(part, cols):
    rows = part.shape[2]
    whole = lax.all_gather(part, "z", axis=0)[..., :cols]
    return whole.transpose(1, 0, 2, 3, 4).reshape(64 * rows, cols)


def xy_parts(grad):
    total_rows, cols = grad.shape
    rows = total_rows // 64
    parts = grad.reshape(2, 8, 4, rows, cols).transpose(0, 2, 1, 3, 4)
    return parts.reshape(8, 8, rows, cols)


def scatter_z(grad):
    total_rows, cols = grad.shape
    rows = total_rows // 64
    parts = grad.reshape(2, 8, 4, rows, cols).transpose(1, 0, 2, 3, 4)
    return lax.psum_scatter(
        parts.reshape(8, 8 * rows, cols), "z", scatter_dimension=0, tiled=False
    ).reshape(8, rows, cols)


def tensor_scatter(product):
    core = lax.axis_index("core")
    high = lax.axis_index("xh")

    def block(xh, c):
        return product(2 * xh + c)

    far_got = peer(block(1 - high, 1 - core).astype(bf16), "core", 1)
    own_got = peer(block(high, 1 - core).astype(bf16), "core", 1)
    away = block(1 - high, core) + far_got.astype(f32)
    away = away.astype(bf16)
    away_got = peer(away, "xh", 1)
    return block(high, core) + own_got.astype(f32) + away_got.astype(f32), away


def row_block(table, index):
    width = table.shape[0] // 4
    return lax.dynamic_slice_in_dim(table, index * width, width, 0)


def tensor_blocks(part):
    beside = peer(part, "core", 1)
    across = peer(part, "xh", 1)
    corner = peer(across, "core", 1)
    return quad_in_order([part, beside, across, corner], lax.axis_index(TENSOR))


def tensor_gather(part):
    return jnp.concatenate(tensor_blocks(part), axis=1)


def body(
    hidden,
    branch,
    up_grad,
    timesteps,
    w_time,
    w_gate,
    w_in,
    w_mid,
    w_out,
    enc_stream,
    enc_attn,
    enc_proj,
    layer_scale,
    enc_gain,
    enc_bias,
    patch_index,
):
    tensor_index = lax.axis_index(TENSOR)
    data_index = lax.axis_index(DP)
    token_rows = hidden.shape[0]
    image_count = timesteps.shape[0]
    image_index = data_index * token_rows // SEQ

    t_freq = time_features(timesteps)
    steps_all = jax.nn.silu(jnp.dot(t_freq, w_time, preferred_element_type=jnp.float32)).astype(
        jnp.bfloat16
    )
    gate_share_rows = w_gate.shape[0]
    own_emb_cols = lax.dynamic_slice_in_dim(
        steps_all, data_index * gate_share_rows, gate_share_rows, 1
    )
    gate_partial = jnp.dot(own_emb_cols, w_gate, preferred_element_type=jnp.float32)
    model_share = w_gate.shape[1]
    in_rows, hidden_share = w_in.shape
    by_image = halves(gate_partial.reshape(2, 2, model_share)).transpose(2, 0, 1, 3)
    gate_rows = pad_to(by_image.reshape(2, 6, hidden_share), (2, 16, hidden_share))
    from_z = exchange(
        jnp.concatenate(
            [
                jnp.broadcast_to(w_in[None], (8, in_rows, hidden_share)),
                jnp.repeat(gate_rows, 4, axis=0),
            ],
            axis=1,
        ),
        "z",
    )

    enc_width = enc_stream.shape[1]
    enc_share = enc_width // 4
    enc_start = tensor_index * enc_share
    projected, _ = tensor_scatter(
        lambda t: jnp.dot(
            enc_attn,
            lax.dynamic_slice_in_dim(enc_proj, t * enc_share, enc_share, 1),
            preferred_element_type=jnp.float32,
        )
    )

    out_share = w_out.shape[1]
    both_tables = gather_xy(
        jnp.pad(jnp.concatenate([w_mid.T, w_out], axis=1), ((0, 0), (0, hidden_share - out_share)))
    )
    both_tables = after(both_tables, from_z)
    from_z, projected = lax.optimization_barrier((from_z, projected))
    gate_by_z = jnp.sum(
        jnp.sum(from_z[:, in_rows : in_rows + 6].astype(f32), axis=0).reshape(2, 2, model_share),
        axis=0,
    )
    gate_rows = pad_to(
        halves(gate_by_z).transpose(1, 0, 2).reshape(2, 3, hidden_share), (2, 16, hidden_share)
    )
    rows_by_z = 8 * in_rows
    from_xy = exchange(
        jnp.concatenate(
            [
                jnp.broadcast_to(
                    from_z[:, :in_rows].reshape(1, rows_by_z, hidden_share),
                    (8, rows_by_z, hidden_share),
                ),
                jnp.repeat(gate_rows, 4, axis=0),
            ],
            axis=1,
        ),
        ("xl", "y"),
    )
    gate_cols = jnp.sum(
        jnp.sum(from_xy[:, rows_by_z : rows_by_z + 3].astype(f32), axis=0).reshape(2, model_share),
        axis=0,
        keepdims=True,
    )
    gate_all = lax.all_gather(gate_cols, TENSOR, axis=1, tiled=True)
    in_table = (
        from_xy[:, :rows_by_z]
        .reshape(2, 4, 8, in_rows, hidden_share)
        .transpose(0, 2, 1, 3, 4)
        .reshape(64 * in_rows, hidden_share)
    )
    mid_turned = gather_z(both_tables[..., :hidden_share], hidden_share)
    out_table = gather_z(both_tables[..., hidden_share:], out_share)

    def own_cols(values):
        return lax.dynamic_slice_in_dim(values, enc_start, enc_share, values.ndim - 1)

    gain, bias = own_cols(enc_gain), own_cols(enc_bias)
    stream = own_cols(enc_stream).astype(f32) + own_cols(layer_scale) * projected
    local_mean = jnp.mean(stream, axis=1)
    local = stream - local_mean[:, None]
    gained = gain * local
    moments = jnp.stack(
        [
            local_mean,
            jnp.sum(local * local, axis=1),
            jnp.sum(gained * gained, axis=1),
            jnp.sum(gained * gain, axis=1),
            jnp.sum(gained * bias, axis=1),
        ]
    )
    block_out = (hidden.astype(jnp.float32) + gate_all * branch.astype(jnp.float32)).astype(
        jnp.bfloat16
    )
    pre_one = jnp.dot(block_out, in_table, preferred_element_type=jnp.float32)
    act_one = jax.nn.silu(pre_one).astype(jnp.bfloat16)
    shared = after(jnp.stack([moments] + peers(moments, TENSOR)), act_one)
    sharer = tensor_index ^ jnp.arange(4, dtype=jnp.int32)

    def share_sums(values):
        return jnp.take(jnp.sum(values.reshape(4, enc_share), axis=1), sharer)[:, None]

    means = shared[:, 0]
    centre = jnp.mean(means, axis=0)
    offs = means - centre
    variance = (jnp.sum(shared[:, 1], axis=0) + enc_share * jnp.sum(offs * offs, axis=0)) / enc_width
    rstd = lax.rsqrt(variance + eps_norm)
    quad = jnp.sum(
        shared[:, 2] + offs * (2.0 * shared[:, 3] + offs * share_sums(enc_gain * enc_gain)), axis=0
    )
    cross = jnp.sum(shared[:, 4] + offs * share_sums(enc_gain * enc_bias), axis=0)
    length = rstd * (rstd * quad + 2.0 * cross) + jnp.sum(enc_bias * enc_bias)
    normed = (stream - centre[:, None]) * rstd[:, None] * gain + bias
    own_unit = (normed * lax.rsqrt(jnp.maximum(length, 0.0) + eps_norm)[:, None]).astype(bf16)
    pre_two, _ = tensor_scatter(
        lambda t: contract_cols(act_one, row_block(mid_turned, t))
    )
    received = lax.all_to_all(own_unit, DP, split_axis=0, concat_axis=0, tiled=True)
    aligned = jnp.take(received, patch_index, axis=0).astype(jnp.float32)
    act_two = tensor_gather(jax.nn.silu(pre_two).astype(jnp.bfloat16))
    proj_out = jnp.dot(act_two, out_table, preferred_element_type=jnp.float32)
    square_sum, inner_sum = lax.psum(
        (jnp.sum(proj_out * proj_out, axis=1), jnp.sum(proj_out * aligned, axis=1)), TENSOR
    )
    inv_len = lax.rsqrt(square_sum + eps_norm)[:, None]
    inner_col = inner_sum[:, None]
    d_out = (
        -loss_scale * (aligned * inv_len - inner_col * inv_len * inv_len * inv_len * proj_out)
    ).astype(jnp.bfloat16)

    back, back_away = tensor_scatter(lambda t: contract_cols(d_out, row_block(out_table, t)))
    d_two = tensor_gather((back * silu_slope(pre_two)).astype(jnp.bfloat16))
    out_by_z = scatter_z(contract_rows(act_two, after(d_out, back_away)).astype(bf16))
    d_one = (
        jnp.dot(d_two, mid_turned, preferred_element_type=jnp.float32) * silu_slope(pre_one)
    ).astype(jnp.bfloat16)
    mid_by_z = scatter_z(contract_rows(d_two, act_one).astype(bf16))
    grad_in = contract_rows(block_out, d_one).astype(bf16)
    stream_share, _ = tensor_scatter(
        lambda t: contract_cols(d_one, row_block(in_table, t))
    )
    in_by_xy = exchange_sum(xy_parts(grad_in), ("xl", "y")).astype(bf16)
    total_grad = up_grad.astype(jnp.float32) + stream_share
    grad_hidden = total_grad.astype(jnp.bfloat16)
    grad_branch = (gate_cols * total_grad).astype(jnp.bfloat16)
    branch_cols = lax.dynamic_slice_in_dim(
        branch, tensor_index * model_share, model_share, 1
    ).astype(jnp.float32)
    device_sum = jnp.sum(total_grad * branch_cols, axis=0)
    sum_rows = pad_to(halves(device_sum).reshape(3, hidden_share), (16, hidden_share))
    last_z = exchange(
        jnp.concatenate(
            [in_by_xy, jnp.broadcast_to(sum_rows[None], (8, 16, hidden_share))], axis=1
        ),
        "z",
    )
    grad_w_in = jnp.sum(last_z[:, :in_rows].astype(f32), axis=0)
    sums_by_z = jnp.sum(
        last_z[:, in_rows : in_rows + 3].astype(f32).reshape(2, 4, 2, model_share), axis=(1, 2)
    )
    both_rows, both_cols = w_out.shape[0], hidden_share + out_share
    sum_rows = pad_to(halves(sums_by_z).reshape(4, model_share), (16, both_cols))
    last_xy = exchange(
        jnp.concatenate(
            [
                jnp.concatenate([mid_by_z, out_by_z], axis=2),
                jnp.broadcast_to(sum_rows[None], (8, 16, both_cols)),
            ],
            axis=1,
        ),
        ("xl", "y"),
    )
    both_grads = jnp.sum(last_xy[:, :both_rows].astype(f32), axis=0)
    grad_w_mid = both_grads[:, :hidden_share].T
    grad_w_out = both_grads[:, hidden_share:]
    image_sums = jnp.sum(
        last_xy[:, both_rows : both_rows + 4, :model_share]
        .astype(f32)
        .reshape(2, 4, 2, 2, model_share),
        axis=(1, 2),
    ).reshape(image_count, model_share)
    grad_w_gate = lax.dot_general(
        own_emb_cols.astype(jnp.float32),
        image_sums,
        (((0,), (0,)), ((), ())),
        precision=lax.Precision.HIGHEST,
        preferred_element_type=jnp.float32,
    )
    return (grad_hidden, grad_branch, grad_w_gate, grad_w_in, grad_w_mid, grad_w_out)


def solution(mesh):
    split = Mesh(mesh.devices.reshape(2, 8, 4, 2, 2), DP + TENSOR)
    return jax.shard_map(
        body,
        mesh=split,
        in_specs=(
            P(DP, None),
            P(DP, None),
            P(DP, TENSOR),
            P(),
            P(),
            P(DP, TENSOR),
            P(DP, TENSOR),
            P(TENSOR, DP),
            P(DP, TENSOR),
            P(DP, None),
            P(DP, TENSOR),
            P(TENSOR, None),
            P(),
            P(),
            P(),
            P(DP),
        ),
        out_specs=(
            P(DP, TENSOR),
            P(DP, TENSOR),
            P(DP, TENSOR),
            P(DP, TENSOR),
            P(TENSOR, DP),
            P(DP, TENSOR),
        ),
        check_vma=False,
    )
```

```python
import math

import jax
import jax.numpy as jnp
from jax import lax
from jax.sharding import Mesh
from jax.sharding import PartitionSpec as P

FREQ = 256
SEQ = 4096
DP = ("xl", "z", "y")
TENSOR = ("xh", "core")

eps_norm = 1e-06
loss_scale = 1024.0
bf16 = jnp.bfloat16
f32 = jnp.float32


def silu_slope(values):
    sigmoid_part = jax.nn.sigmoid(values)
    return sigmoid_part * (1.0 + values * (1.0 - sigmoid_part))


def time_features(timesteps):
    half_freq = FREQ // 2
    frequency = jnp.exp(-math.log(10000.0) * jnp.arange(half_freq, dtype=jnp.float32) / half_freq)
    angles = timesteps.astype(jnp.float32)[:, None] * frequency[None, :]
    return jnp.concatenate([jnp.cos(angles), jnp.sin(angles)], axis=1).astype(jnp.bfloat16)


def contract_rows(left, right):
    return lax.dot_general(
        left, right, (((0,), (0,)), ((), ())), preferred_element_type=jnp.float32
    )


def contract_cols(left, right):
    return lax.dot_general(
        left, right, (((1,), (1,)), ((), ())), preferred_element_type=jnp.float32
    )


def peer(value, axis, bits):
    count = lax.axis_size(axis)
    return lax.ppermute(value, axis, [(i, i ^ bits) for i in range(count)])


def peers(value, axis):
    return [peer(value, axis, bits) for bits in (1, 2, 3)]


def together(*values):
    return lax.optimization_barrier(values)


def pick(values, index, axis=0):
    return lax.dynamic_index_in_dim(values, index, axis, keepdims=False)


def pair_in_order(own, other, first):
    return [jnp.where(first, own, other), jnp.where(first, other, own)]


def quad_in_order(blocks, index):
    near = pair_in_order(blocks[0], blocks[1], index % 2 == 0)
    far = pair_in_order(blocks[2], blocks[3], index % 2 == 0)
    low_first = index < 2
    return [jnp.where(low_first, a, b) for a, b in zip(near, far)] + [
        jnp.where(low_first, b, a) for a, b in zip(near, far)
    ]


def halves(value):
    high = lax.reduce_precision(value, 8, 7)
    return jnp.stack([high.astype(bf16), (value - high).astype(bf16)])


def pad_to(value, shape):
    return jnp.pad(value, [(0, full - own) for own, full in zip(value.shape, shape)])


def exchange(parts, axes):
    return lax.all_to_all(parts, axes, 0, 0, tiled=True)


def exchange_sum(parts, axes):
    got = lax.all_to_all(parts.astype(bf16), axes, 0, 0, tiled=True)
    return jnp.sum(got.astype(f32), axis=0)


def gather_xy(part):
    pair = jnp.stack(pair_in_order(part, peer(part, "xl", 1), lax.axis_index("xl") == 0))
    quad = quad_in_order([pair] + peers(pair, "y"), lax.axis_index("y"))
    return jnp.stack(quad, axis=1)


def gather_z(part, cols):
    rows = part.shape[2]
    whole = lax.all_gather(part, "z", axis=0)[..., :cols]
    return whole.transpose(1, 0, 2, 3, 4).reshape(64 * rows, cols)


def xy_parts(grad):
    total_rows, cols = grad.shape
    rows = total_rows // 64
    parts = grad.reshape(2, 8, 4, rows, cols).transpose(0, 2, 1, 3, 4)
    return parts.reshape(8, 8, rows, cols)


def scatter_z(grad):
    total_rows, cols = grad.shape
    rows = total_rows // 64
    parts = grad.reshape(2, 8, 4, rows, cols).transpose(1, 0, 2, 3, 4)
    return lax.psum_scatter(
        parts.reshape(8, 8 * rows, cols), "z", scatter_dimension=0, tiled=False
    ).reshape(8, rows, cols)


def tensor_scatter(product):
    core = lax.axis_index("core")
    high = lax.axis_index("xh")

    def block(xh, c):
        return product(2 * xh + c)

    far_got = peer(block(1 - high, 1 - core).astype(bf16), "core", 1)
    own_got = peer(block(high, 1 - core).astype(bf16), "core", 1)
    away = block(1 - high, core) + far_got.astype(f32)
    away = away.astype(bf16)
    away_got = peer(away, "xh", 1)
    return block(high, core) + own_got.astype(f32) + away_got.astype(f32)


def row_block(table, index):
    width = table.shape[0] // 4
    return lax.dynamic_slice_in_dim(table, index * width, width, 0)


def tensor_blocks(part):
    beside = peer(part, "core", 1)
    across = peer(part, "xh", 1)
    corner = peer(across, "core", 1)
    return quad_in_order([part, beside, across, corner], lax.axis_index(TENSOR))


def tensor_gather(part):
    return jnp.concatenate(tensor_blocks(part), axis=1)


def body(
    hidden,
    branch,
    up_grad,
    timesteps,
    w_time,
    w_gate,
    w_in,
    w_mid,
    w_out,
    enc_stream,
    enc_attn,
    enc_proj,
    layer_scale,
    enc_gain,
    enc_bias,
    patch_index,
):
    tensor_index = lax.axis_index(TENSOR)
    data_index = lax.axis_index(DP)
    token_rows = hidden.shape[0]
    image_count = timesteps.shape[0]
    image_index = data_index * token_rows // SEQ

    t_freq = time_features(timesteps)
    steps_all = jax.nn.silu(jnp.dot(t_freq, w_time, preferred_element_type=jnp.float32)).astype(
        jnp.bfloat16
    )
    gate_share_rows = w_gate.shape[0]
    own_emb_cols = lax.dynamic_slice_in_dim(
        steps_all, data_index * gate_share_rows, gate_share_rows, 1
    )
    gate_partial = jnp.dot(own_emb_cols, w_gate, preferred_element_type=jnp.float32)
    model_share = w_gate.shape[1]
    in_rows, hidden_share = w_in.shape
    by_image = halves(gate_partial.reshape(2, 2, model_share)).transpose(2, 0, 1, 3)
    gate_rows = pad_to(by_image.reshape(2, 6, hidden_share), (2, 16, hidden_share))
    from_z = exchange(
        jnp.concatenate(
            [
                jnp.broadcast_to(w_in[None], (8, in_rows, hidden_share)),
                jnp.repeat(gate_rows, 4, axis=0),
            ],
            axis=1,
        ),
        "z",
    )

    enc_width = enc_stream.shape[1]
    enc_share = enc_width // 4
    enc_start = tensor_index * enc_share
    projected = tensor_scatter(
        lambda t: jnp.dot(
            enc_attn,
            lax.dynamic_slice_in_dim(enc_proj, t * enc_share, enc_share, 1),
            preferred_element_type=jnp.float32,
        )
    )

    out_share = w_out.shape[1]
    both_tables = gather_xy(
        jnp.pad(jnp.concatenate([w_mid.T, w_out], axis=1), ((0, 0), (0, hidden_share - out_share))),
    )
    both_tables, from_z, projected = together(both_tables, from_z, projected)
    gate_by_z = jnp.sum(
        jnp.sum(from_z[:, in_rows : in_rows + 6].astype(f32), axis=0).reshape(2, 2, model_share),
        axis=0,
    )
    gate_by_z = lax.all_gather(gate_by_z, TENSOR, axis=1, tiled=True)
    gate_rows = pad_to(
        halves(gate_by_z).transpose(1, 0, 2).reshape(2, 12, hidden_share), (2, 16, hidden_share)
    )
    rows_by_z = 8 * in_rows
    from_xy = exchange(
        jnp.concatenate(
            [
                jnp.broadcast_to(
                    from_z[:, :in_rows].reshape(1, rows_by_z, hidden_share),
                    (8, rows_by_z, hidden_share),
                ),
                jnp.repeat(gate_rows, 4, axis=0),
            ],
            axis=1,
        ),
        ("xl", "y"),
    )
    gate_all = jnp.sum(
        jnp.sum(from_xy[:, rows_by_z : rows_by_z + 12].astype(f32), axis=0).reshape(
            2, 4 * model_share
        ),
        axis=0,
        keepdims=True,
    )
    gate_cols = lax.dynamic_slice_in_dim(gate_all, tensor_index * model_share, model_share, 1)
    in_table = (
        from_xy[:, :rows_by_z]
        .reshape(2, 4, 8, in_rows, hidden_share)
        .transpose(0, 2, 1, 3, 4)
        .reshape(64 * in_rows, hidden_share)
    )
    mid_turned = gather_z(both_tables[..., :hidden_share], hidden_share)
    out_table = gather_z(both_tables[..., hidden_share:], out_share)

    def own_cols(values):
        return lax.dynamic_slice_in_dim(values, enc_start, enc_share, values.ndim - 1)

    gain, bias = own_cols(enc_gain), own_cols(enc_bias)
    stream = own_cols(enc_stream).astype(f32) + own_cols(layer_scale) * projected
    local_mean = jnp.mean(stream, axis=1)
    local = stream - local_mean[:, None]
    gained = gain * local
    moments = jnp.stack(
        [
            local_mean,
            jnp.sum(local * local, axis=1),
            jnp.sum(gained * gained, axis=1),
            jnp.sum(gained * gain, axis=1),
            jnp.sum(gained * bias, axis=1),
        ]
    )

    block_out = (hidden.astype(jnp.float32) + gate_all * branch.astype(jnp.float32)).astype(
        jnp.bfloat16
    )
    pre_one = jnp.dot(block_out, in_table, preferred_element_type=jnp.float32)
    act_one = jax.nn.silu(pre_one).astype(jnp.bfloat16)
    shared = jnp.stack([moments] + peers(moments, TENSOR))
    sharer = tensor_index ^ jnp.arange(4, dtype=jnp.int32)

    def share_sums(values):
        return jnp.take(jnp.sum(values.reshape(4, enc_share), axis=1), sharer)[:, None]

    means = shared[:, 0]
    centre = jnp.mean(means, axis=0)
    offs = means - centre
    variance = (jnp.sum(shared[:, 1], axis=0) + enc_share * jnp.sum(offs * offs, axis=0)) / enc_width
    rstd = lax.rsqrt(variance + eps_norm)
    quad = jnp.sum(
        shared[:, 2] + offs * (2.0 * shared[:, 3] + offs * share_sums(enc_gain * enc_gain)), axis=0
    )
    cross = jnp.sum(shared[:, 4] + offs * share_sums(enc_gain * enc_bias), axis=0)
    length = rstd * (rstd * quad + 2.0 * cross) + jnp.sum(enc_bias * enc_bias)
    normed = (stream - centre[:, None]) * rstd[:, None] * gain + bias
    own_unit = (normed * lax.rsqrt(jnp.maximum(length, 0.0) + eps_norm)[:, None]).astype(bf16)
    pre_two = tensor_scatter(
        lambda t: contract_cols(act_one, row_block(mid_turned, t))
    )
    received = lax.all_to_all(own_unit, DP, split_axis=0, concat_axis=0, tiled=True)
    aligned = jnp.take(received, patch_index, axis=0).astype(jnp.float32)
    act_two = tensor_gather(jax.nn.silu(pre_two).astype(jnp.bfloat16))
    proj_out = jnp.dot(act_two, out_table, preferred_element_type=jnp.float32)
    square_sum, inner_sum = lax.psum(
        (jnp.sum(proj_out * proj_out, axis=1), jnp.sum(proj_out * aligned, axis=1)), TENSOR
    )
    inv_len = lax.rsqrt(square_sum + eps_norm)[:, None]
    inner_col = inner_sum[:, None]
    d_out = (
        -loss_scale * (aligned * inv_len - inner_col * inv_len * inv_len * inv_len * proj_out)
    ).astype(jnp.bfloat16)

    grad_out, d_out = together(contract_rows(act_two, d_out).astype(bf16), d_out)
    out_by_z = scatter_z(grad_out)
    back = tensor_scatter(lambda t: contract_cols(d_out, row_block(out_table, t)))
    d_two = tensor_gather((back * silu_slope(pre_two)).astype(jnp.bfloat16))
    d_one = (
        jnp.dot(d_two, mid_turned, preferred_element_type=jnp.float32) * silu_slope(pre_one)
    ).astype(jnp.bfloat16)
    mid_by_xy = exchange_sum(
        xy_parts(contract_rows(d_two, act_one).astype(bf16)), ("xl", "y")
    ).astype(bf16)
    in_by_z = scatter_z(contract_rows(block_out, d_one).astype(bf16))
    stream_share = tensor_scatter(
        lambda t: contract_cols(d_one, row_block(in_table, t))
    )
    total_grad = up_grad.astype(jnp.float32) + stream_share
    grad_hidden = total_grad.astype(jnp.bfloat16)
    grad_branch = (gate_cols * total_grad).astype(jnp.bfloat16)
    branch_cols = lax.dynamic_slice_in_dim(
        branch, tensor_index * model_share, model_share, 1
    ).astype(jnp.float32)
    device_sum = jnp.sum(total_grad * branch_cols, axis=0)
    mid_rows = mid_by_xy.shape[1]
    sum_rows = pad_to(halves(device_sum).reshape(3, hidden_share), (16, hidden_share))
    last_z = exchange(
        jnp.concatenate(
            [mid_by_xy, jnp.broadcast_to(sum_rows[None], (8, 16, hidden_share))], axis=1
        ),
        "z",
    )
    grad_w_mid = jnp.sum(last_z[:, :mid_rows].astype(f32), axis=0).T
    sums_by_z = jnp.sum(
        last_z[:, mid_rows : mid_rows + 3].astype(f32).reshape(2, 4, 2, model_share), axis=(1, 2)
    )
    sum_rows = pad_to(halves(sums_by_z).reshape(6, hidden_share), (16, hidden_share))
    last_xy = exchange(
        jnp.concatenate(
            [
                in_by_z,
                jnp.broadcast_to(sum_rows[None], (8, 16, hidden_share)),
                pad_to(out_by_z, (8, out_by_z.shape[1], hidden_share)),
            ],
            axis=1,
        ),
        ("xl", "y"),
    )
    grad_w_in = jnp.sum(last_xy[:, :in_rows].astype(f32), axis=0)
    grad_w_out = jnp.sum(last_xy[:, in_rows + 16 :, :out_share].astype(f32), axis=0)
    image_sums = jnp.sum(
        last_xy[:, in_rows : in_rows + 6].astype(f32).reshape(2, 4, 2, 2, model_share),
        axis=(1, 2),
    ).reshape(image_count, model_share)
    grad_w_gate = lax.dot_general(
        own_emb_cols.astype(jnp.float32),
        image_sums,
        (((0,), (0,)), ((), ())),
        precision=lax.Precision.HIGHEST,
        preferred_element_type=jnp.float32,
    )
    return (grad_hidden, grad_branch, grad_w_gate, grad_w_in, grad_w_mid, grad_w_out)


def solution(mesh):
    split = Mesh(mesh.devices.reshape(2, 8, 4, 2, 2), DP + TENSOR)
    return jax.shard_map(
        body,
        mesh=split,
        in_specs=(
            P(DP, None),
            P(DP, None),
            P(DP, TENSOR),
            P(),
            P(),
            P(DP, TENSOR),
            P(DP, TENSOR),
            P(TENSOR, DP),
            P(DP, TENSOR),
            P(DP, None),
            P(DP, TENSOR),
            P(TENSOR, None),
            P(),
            P(),
            P(),
            P(DP),
        ),
        out_specs=(
            P(DP, TENSOR),
            P(DP, TENSOR),
            P(DP, TENSOR),
            P(DP, TENSOR),
            P(TENSOR, DP),
            P(DP, TENSOR),
        ),
        check_vma=False,
    )
```

```python
import math

import jax
import jax.numpy as jnp
from jax import lax
from jax.sharding import Mesh
from jax.sharding import PartitionSpec as P

FREQ = 256
SEQ = 4096
DP = ("xl", "z", "y")
TENSOR = ("xh", "core")

eps_norm = 1e-06
loss_scale = 1024.0
bf16 = jnp.bfloat16
f32 = jnp.float32


def silu_slope(values):
    sigmoid_part = jax.nn.sigmoid(values)
    return sigmoid_part * (1.0 + values * (1.0 - sigmoid_part))


def time_features(timesteps):
    half_freq = FREQ // 2
    frequency = jnp.exp(-math.log(10000.0) * jnp.arange(half_freq, dtype=jnp.float32) / half_freq)
    angles = timesteps.astype(jnp.float32)[:, None] * frequency[None, :]
    return jnp.concatenate([jnp.cos(angles), jnp.sin(angles)], axis=1).astype(jnp.bfloat16)


def contract_rows(left, right):
    return lax.dot_general(
        left, right, (((0,), (0,)), ((), ())), preferred_element_type=jnp.float32
    )


def contract_cols(left, right):
    return lax.dot_general(
        left, right, (((1,), (1,)), ((), ())), preferred_element_type=jnp.float32
    )


def peer(value, axis, bits):
    count = lax.axis_size(axis)
    return lax.ppermute(value, axis, [(i, i ^ bits) for i in range(count)])


def peers(value, axis):
    return [peer(value, axis, bits) for bits in (1, 2, 3)]


def together(*values):
    return lax.optimization_barrier(values)


def pick(values, index, axis=0):
    return lax.dynamic_index_in_dim(values, index, axis, keepdims=False)


def pair_in_order(own, other, first):
    return [jnp.where(first, own, other), jnp.where(first, other, own)]


def quad_in_order(blocks, index):
    near = pair_in_order(blocks[0], blocks[1], index % 2 == 0)
    far = pair_in_order(blocks[2], blocks[3], index % 2 == 0)
    low_first = index < 2
    return [jnp.where(low_first, a, b) for a, b in zip(near, far)] + [
        jnp.where(low_first, b, a) for a, b in zip(near, far)
    ]


def halves(value):
    high = lax.reduce_precision(value, 8, 7)
    return jnp.stack([high.astype(bf16), (value - high).astype(bf16)])


def pad_to(value, shape):
    return jnp.pad(value, [(0, full - own) for own, full in zip(value.shape, shape)])


def exchange(parts, axes):
    return lax.all_to_all(parts, axes, 0, 0, tiled=True)


def exchange_sum(parts, axes):
    got = lax.all_to_all(parts.astype(bf16), axes, 0, 0, tiled=True)
    return jnp.sum(got.astype(f32), axis=0)


def gather_xy(part):
    pair = jnp.stack(pair_in_order(part, peer(part, "xl", 1), lax.axis_index("xl") == 0))
    quad = quad_in_order([pair] + peers(pair, "y"), lax.axis_index("y"))
    return jnp.stack(quad, axis=1)


def gather_z(part, cols):
    rows = part.shape[2]
    whole = lax.all_gather(part, "z", axis=0)[..., :cols]
    return whole.transpose(1, 0, 2, 3, 4).reshape(64 * rows, cols)


def xy_parts(grad):
    total_rows, cols = grad.shape
    rows = total_rows // 64
    parts = grad.reshape(2, 8, 4, rows, cols).transpose(0, 2, 1, 3, 4)
    return parts.reshape(8, 8, rows, cols)


def scatter_z(grad):
    total_rows, cols = grad.shape
    rows = total_rows // 64
    parts = grad.reshape(2, 8, 4, rows, cols).transpose(1, 0, 2, 3, 4)
    return lax.psum_scatter(
        parts.reshape(8, 8 * rows, cols), "z", scatter_dimension=0, tiled=False
    ).reshape(8, rows, cols)


def tensor_scatter(product):
    core = lax.axis_index("core")
    high = lax.axis_index("xh")

    def block(xh, c):
        return product(2 * xh + c)

    far_got = peer(block(1 - high, 1 - core).astype(bf16), "core", 1)
    own_got = peer(block(high, 1 - core).astype(bf16), "core", 1)
    away = block(1 - high, core) + far_got.astype(f32)
    away = away.astype(bf16)
    away_got = peer(away, "xh", 1)
    return block(high, core) + own_got.astype(f32) + away_got.astype(f32)


def row_block(table, index):
    width = table.shape[0] // 4
    return lax.dynamic_slice_in_dim(table, index * width, width, 0)


def tensor_blocks(part):
    beside = peer(part, "core", 1)
    across = peer(part, "xh", 1)
    corner = peer(across, "core", 1)
    return quad_in_order([part, beside, across, corner], lax.axis_index(TENSOR))


def tensor_gather(part):
    return jnp.concatenate(tensor_blocks(part), axis=1)


def body(
    hidden,
    branch,
    up_grad,
    timesteps,
    w_time,
    w_gate,
    w_in,
    w_mid,
    w_out,
    enc_stream,
    enc_attn,
    enc_proj,
    layer_scale,
    enc_gain,
    enc_bias,
    patch_index,
):
    tensor_index = lax.axis_index(TENSOR)
    data_index = lax.axis_index(DP)
    token_rows = hidden.shape[0]
    image_count = timesteps.shape[0]
    image_index = data_index * token_rows // SEQ

    t_freq = time_features(timesteps)
    steps_all = jax.nn.silu(jnp.dot(t_freq, w_time, preferred_element_type=jnp.float32)).astype(
        jnp.bfloat16
    )
    gate_share_rows = w_gate.shape[0]
    own_emb_cols = lax.dynamic_slice_in_dim(
        steps_all, data_index * gate_share_rows, gate_share_rows, 1
    )
    gate_partial = jnp.dot(own_emb_cols, w_gate, preferred_element_type=jnp.float32)
    model_share = w_gate.shape[1]
    in_rows, hidden_share = w_in.shape
    by_image = halves(gate_partial.reshape(2, 2, model_share)).transpose(2, 0, 1, 3)
    gate_rows = pad_to(by_image.reshape(2, 6, hidden_share), (2, 16, hidden_share))
    to_z = jnp.concatenate(
        [
            jnp.broadcast_to(w_in[None], (8, in_rows, hidden_share)),
            jnp.repeat(gate_rows, 4, axis=0),
        ],
        axis=1,
    )
    to_z, enc_attn, w_out = together(to_z, enc_attn, w_out)
    from_z = exchange(to_z, "z")

    enc_width = enc_stream.shape[1]
    enc_share = enc_width // 4
    enc_start = tensor_index * enc_share
    projected = tensor_scatter(
        lambda t: jnp.dot(
            enc_attn,
            lax.dynamic_slice_in_dim(enc_proj, t * enc_share, enc_share, 1),
            preferred_element_type=jnp.float32,
        )
    )

    out_share = w_out.shape[1]
    both_tables = gather_xy(
        jnp.pad(jnp.concatenate([w_mid.T, w_out], axis=1), ((0, 0), (0, hidden_share - out_share))),
    )
    both_tables, from_z, projected = together(both_tables, from_z, projected)
    gate_by_z = jnp.sum(
        jnp.sum(from_z[:, in_rows : in_rows + 6].astype(f32), axis=0).reshape(2, 2, model_share),
        axis=0,
    )
    gate_by_z = lax.all_gather(gate_by_z, TENSOR, axis=1, tiled=True)
    gate_rows = pad_to(
        halves(gate_by_z).transpose(1, 0, 2).reshape(2, 12, hidden_share), (2, 16, hidden_share)
    )
    rows_by_z = 8 * in_rows
    from_xy = exchange(
        jnp.concatenate(
            [
                jnp.broadcast_to(
                    from_z[:, :in_rows].reshape(1, rows_by_z, hidden_share),
                    (8, rows_by_z, hidden_share),
                ),
                jnp.repeat(gate_rows, 4, axis=0),
            ],
            axis=1,
        ),
        ("xl", "y"),
    )
    gate_all = jnp.sum(
        jnp.sum(from_xy[:, rows_by_z : rows_by_z + 12].astype(f32), axis=0).reshape(
            2, 4 * model_share
        ),
        axis=0,
        keepdims=True,
    )
    gate_cols = lax.dynamic_slice_in_dim(gate_all, tensor_index * model_share, model_share, 1)
    in_table = (
        from_xy[:, :rows_by_z]
        .reshape(2, 4, 8, in_rows, hidden_share)
        .transpose(0, 2, 1, 3, 4)
        .reshape(64 * in_rows, hidden_share)
    )
    mid_turned = gather_z(both_tables[..., :hidden_share], hidden_share)
    out_table = gather_z(both_tables[..., hidden_share:], out_share)

    def own_cols(values):
        return lax.dynamic_slice_in_dim(values, enc_start, enc_share, values.ndim - 1)

    gain, bias = own_cols(enc_gain), own_cols(enc_bias)
    stream = own_cols(enc_stream).astype(f32) + own_cols(layer_scale) * projected
    local_mean = jnp.mean(stream, axis=1)
    local = stream - local_mean[:, None]
    gained = gain * local
    moments = jnp.stack(
        [
            local_mean,
            jnp.sum(local * local, axis=1),
            jnp.sum(gained * gained, axis=1),
            jnp.sum(gained * gain, axis=1),
            jnp.sum(gained * bias, axis=1),
        ]
    )

    block_out = (hidden.astype(jnp.float32) + gate_all * branch.astype(jnp.float32)).astype(
        jnp.bfloat16
    )
    pre_one = jnp.dot(block_out, in_table, preferred_element_type=jnp.float32)
    act_one = jax.nn.silu(pre_one).astype(jnp.bfloat16)
    shared = jnp.stack([moments] + peers(moments, TENSOR))
    sharer = tensor_index ^ jnp.arange(4, dtype=jnp.int32)

    def share_sums(values):
        return jnp.take(jnp.sum(values.reshape(4, enc_share), axis=1), sharer)[:, None]

    means = shared[:, 0]
    centre = jnp.mean(means, axis=0)
    offs = means - centre
    variance = (jnp.sum(shared[:, 1], axis=0) + enc_share * jnp.sum(offs * offs, axis=0)) / enc_width
    rstd = lax.rsqrt(variance + eps_norm)
    quad = jnp.sum(
        shared[:, 2] + offs * (2.0 * shared[:, 3] + offs * share_sums(enc_gain * enc_gain)), axis=0
    )
    cross = jnp.sum(shared[:, 4] + offs * share_sums(enc_gain * enc_bias), axis=0)
    length = rstd * (rstd * quad + 2.0 * cross) + jnp.sum(enc_bias * enc_bias)
    normed = (stream - centre[:, None]) * rstd[:, None] * gain + bias
    own_unit = (normed * lax.rsqrt(jnp.maximum(length, 0.0) + eps_norm)[:, None]).astype(bf16)
    pre_two = tensor_scatter(
        lambda t: contract_cols(act_one, row_block(mid_turned, t))
    )
    received = lax.all_to_all(own_unit, DP, split_axis=0, concat_axis=0, tiled=True)
    aligned = jnp.take(received, patch_index, axis=0).astype(jnp.float32)
    act_two = tensor_gather(jax.nn.silu(pre_two).astype(jnp.bfloat16))
    proj_out = jnp.dot(act_two, out_table, preferred_element_type=jnp.float32)
    square_sum, inner_sum = lax.psum(
        (jnp.sum(proj_out * proj_out, axis=1), jnp.sum(proj_out * aligned, axis=1)), TENSOR
    )
    inv_len = lax.rsqrt(square_sum + eps_norm)[:, None]
    inner_col = inner_sum[:, None]
    d_out = (
        -loss_scale * (aligned * inv_len - inner_col * inv_len * inv_len * inv_len * proj_out)
    ).astype(jnp.bfloat16)

    grad_out, d_out = together(contract_rows(act_two, d_out).astype(bf16), d_out)
    out_by_z = scatter_z(grad_out)
    back = tensor_scatter(lambda t: contract_cols(d_out, row_block(out_table, t)))
    d_two = tensor_gather((back * silu_slope(pre_two)).astype(jnp.bfloat16))
    d_one = (
        jnp.dot(d_two, mid_turned, preferred_element_type=jnp.float32) * silu_slope(pre_one)
    ).astype(jnp.bfloat16)
    mid_by_xy = exchange_sum(
        xy_parts(contract_rows(d_two, act_one).astype(bf16)), ("xl", "y")
    ).astype(bf16)
    in_by_z = scatter_z(contract_rows(block_out, d_one).astype(bf16))
    stream_share = tensor_scatter(
        lambda t: contract_cols(d_one, row_block(in_table, t))
    )
    total_grad = up_grad.astype(jnp.float32) + stream_share
    grad_hidden = total_grad.astype(jnp.bfloat16)
    grad_branch = (gate_cols * total_grad).astype(jnp.bfloat16)
    branch_cols = lax.dynamic_slice_in_dim(
        branch, tensor_index * model_share, model_share, 1
    ).astype(jnp.float32)
    device_sum = jnp.sum(total_grad * branch_cols, axis=0)
    mid_rows = mid_by_xy.shape[1]
    sum_rows = pad_to(halves(device_sum).reshape(3, hidden_share), (16, hidden_share))
    last_z = exchange(
        jnp.concatenate(
            [mid_by_xy, jnp.broadcast_to(sum_rows[None], (8, 16, hidden_share))], axis=1
        ),
        "z",
    )
    grad_w_mid = jnp.sum(last_z[:, :mid_rows].astype(f32), axis=0).T
    sums_by_z = jnp.sum(
        last_z[:, mid_rows : mid_rows + 3].astype(f32).reshape(2, 4, 2, model_share), axis=(1, 2)
    )
    sum_rows = pad_to(halves(sums_by_z).reshape(6, hidden_share), (16, hidden_share))
    last_xy = exchange(
        jnp.concatenate(
            [
                in_by_z,
                jnp.broadcast_to(sum_rows[None], (8, 16, hidden_share)),
                pad_to(out_by_z, (8, out_by_z.shape[1], hidden_share)),
            ],
            axis=1,
        ),
        ("xl", "y"),
    )
    grad_w_in = jnp.sum(last_xy[:, :in_rows].astype(f32), axis=0)
    grad_w_out = jnp.sum(last_xy[:, in_rows + 16 :, :out_share].astype(f32), axis=0)
    image_sums = jnp.sum(
        last_xy[:, in_rows : in_rows + 6].astype(f32).reshape(2, 4, 2, 2, model_share),
        axis=(1, 2),
    ).reshape(image_count, model_share)
    grad_w_gate = lax.dot_general(
        own_emb_cols.astype(jnp.float32),
        image_sums,
        (((0,), (0,)), ((), ())),
        precision=lax.Precision.HIGHEST,
        preferred_element_type=jnp.float32,
    )
    return (grad_hidden, grad_branch, grad_w_gate, grad_w_in, grad_w_mid, grad_w_out)


def solution(mesh):
    split = Mesh(mesh.devices.reshape(2, 8, 4, 2, 2), DP + TENSOR)
    return jax.shard_map(
        body,
        mesh=split,
        in_specs=(
            P(DP, None),
            P(DP, None),
            P(DP, TENSOR),
            P(),
            P(),
            P(DP, TENSOR),
            P(DP, TENSOR),
            P(TENSOR, DP),
            P(DP, TENSOR),
            P(DP, None),
            P(DP, TENSOR),
            P(TENSOR, None),
            P(),
            P(),
            P(),
            P(DP),
        ),
        out_specs=(
            P(DP, TENSOR),
            P(DP, TENSOR),
            P(DP, TENSOR),
            P(DP, TENSOR),
            P(TENSOR, DP),
            P(DP, TENSOR),
        ),
        check_vma=False,
    )
```

```python
import math

import jax
import jax.numpy as jnp
from jax import lax
from jax.sharding import Mesh
from jax.sharding import PartitionSpec as P

FREQ = 256
SEQ = 4096
DP = ("xl", "z", "y")
TENSOR = ("xh", "core")

eps_norm = 1e-06
loss_scale = 1024.0
bf16 = jnp.bfloat16
f32 = jnp.float32


def silu_slope(values):
    sigmoid_part = jax.nn.sigmoid(values)
    return sigmoid_part * (1.0 + values * (1.0 - sigmoid_part))


def time_features(timesteps):
    half_freq = FREQ // 2
    frequency = jnp.exp(-math.log(10000.0) * jnp.arange(half_freq, dtype=jnp.float32) / half_freq)
    angles = timesteps.astype(jnp.float32)[:, None] * frequency[None, :]
    return jnp.concatenate([jnp.cos(angles), jnp.sin(angles)], axis=1).astype(jnp.bfloat16)


def contract_rows(left, right):
    return lax.dot_general(
        left, right, (((0,), (0,)), ((), ())), preferred_element_type=jnp.float32
    )


def contract_cols(left, right):
    return lax.dot_general(
        left, right, (((1,), (1,)), ((), ())), preferred_element_type=jnp.float32
    )


def peer(value, axis, bits):
    count = lax.axis_size(axis)
    return lax.ppermute(value, axis, [(i, i ^ bits) for i in range(count)])


def peers(value, axis):
    return [peer(value, axis, bits) for bits in (1, 2, 3)]


def together(*values):
    return lax.optimization_barrier(values)


def pick(values, index, axis=0):
    return lax.dynamic_index_in_dim(values, index, axis, keepdims=False)


def pair_in_order(own, other, first):
    return [jnp.where(first, own, other), jnp.where(first, other, own)]


def quad_in_order(blocks, index):
    near = pair_in_order(blocks[0], blocks[1], index % 2 == 0)
    far = pair_in_order(blocks[2], blocks[3], index % 2 == 0)
    low_first = index < 2
    return [jnp.where(low_first, a, b) for a, b in zip(near, far)] + [
        jnp.where(low_first, b, a) for a, b in zip(near, far)
    ]


def halves(value):
    high = lax.reduce_precision(value, 8, 7)
    return jnp.stack([high.astype(bf16), (value - high).astype(bf16)])


def pad_to(value, shape):
    return jnp.pad(value, [(0, full - own) for own, full in zip(value.shape, shape)])


def exchange(parts, axes):
    return lax.all_to_all(parts, axes, 0, 0, tiled=True)


def exchange_sum(parts, axes):
    got = lax.all_to_all(parts.astype(bf16), axes, 0, 0, tiled=True)
    return jnp.sum(got.astype(f32), axis=0)


def gather_xy(part):
    pair = jnp.stack(pair_in_order(part, peer(part, "xl", 1), lax.axis_index("xl") == 0))
    quad = quad_in_order([pair] + peers(pair, "y"), lax.axis_index("y"))
    return jnp.stack(quad, axis=1)


def gather_z(part, cols):
    rows = part.shape[2]
    whole = lax.all_gather(part, "z", axis=0)[..., :cols]
    return whole.transpose(1, 0, 2, 3, 4).reshape(64 * rows, cols)


def xy_parts(grad):
    total_rows, cols = grad.shape
    rows = total_rows // 64
    parts = grad.reshape(2, 8, 4, rows, cols).transpose(0, 2, 1, 3, 4)
    return parts.reshape(8, 8, rows, cols)


def scatter_z(grad):
    total_rows, cols = grad.shape
    rows = total_rows // 64
    parts = grad.reshape(2, 8, 4, rows, cols).transpose(1, 0, 2, 3, 4)
    return lax.psum_scatter(
        parts.reshape(8, 8 * rows, cols), "z", scatter_dimension=0, tiled=False
    ).reshape(8, rows, cols)


def tensor_scatter(product):
    core = lax.axis_index("core")
    high = lax.axis_index("xh")

    def block(xh, c):
        return product(2 * xh + c)

    far_got = peer(block(1 - high, 1 - core).astype(bf16), "core", 1)
    own_got = peer(block(high, 1 - core).astype(bf16), "core", 1)
    away = block(1 - high, core) + far_got.astype(f32)
    away = away.astype(bf16)
    away_got = peer(away, "xh", 1)
    return block(high, core) + own_got.astype(f32) + away_got.astype(f32)


def row_block(table, index):
    width = table.shape[0] // 4
    return lax.dynamic_slice_in_dim(table, index * width, width, 0)


def tensor_blocks(part):
    beside = peer(part, "core", 1)
    across = peer(part, "xh", 1)
    corner = peer(across, "core", 1)
    return quad_in_order([part, beside, across, corner], lax.axis_index(TENSOR))


def tensor_gather(part):
    return jnp.concatenate(tensor_blocks(part), axis=1)


def body(
    hidden,
    branch,
    up_grad,
    timesteps,
    w_time,
    w_gate,
    w_in,
    w_mid,
    w_out,
    enc_stream,
    enc_attn,
    enc_proj,
    layer_scale,
    enc_gain,
    enc_bias,
    patch_index,
):
    tensor_index = lax.axis_index(TENSOR)
    data_index = lax.axis_index(DP)
    token_rows = hidden.shape[0]
    image_count = timesteps.shape[0]
    image_index = data_index * token_rows // SEQ

    t_freq = time_features(timesteps)
    steps_all = jax.nn.silu(jnp.dot(t_freq, w_time, preferred_element_type=jnp.float32)).astype(
        jnp.bfloat16
    )
    gate_share_rows = w_gate.shape[0]
    own_emb_cols = lax.dynamic_slice_in_dim(
        steps_all, data_index * gate_share_rows, gate_share_rows, 1
    )
    gate_partial = jnp.dot(own_emb_cols, w_gate, preferred_element_type=jnp.float32)
    model_share = w_gate.shape[1]
    in_rows, hidden_share = w_in.shape
    by_image = halves(gate_partial.reshape(2, 2, model_share)).transpose(2, 0, 1, 3)
    gate_rows = pad_to(by_image.reshape(2, 6, hidden_share), (2, 16, hidden_share))
    to_z = jnp.concatenate(
        [
            jnp.broadcast_to(w_in[None], (8, in_rows, hidden_share)),
            jnp.repeat(gate_rows, 4, axis=0),
        ],
        axis=1,
    )
    to_z, enc_attn, w_out = together(to_z, enc_attn, w_out)
    from_z = exchange(to_z, "z")

    enc_width = enc_stream.shape[1]
    enc_share = enc_width // 4
    enc_start = tensor_index * enc_share
    projected = tensor_scatter(
        lambda t: jnp.dot(
            enc_attn,
            lax.dynamic_slice_in_dim(enc_proj, t * enc_share, enc_share, 1),
            preferred_element_type=jnp.float32,
        )
    )

    out_share = w_out.shape[1]
    both_tables = gather_xy(
        jnp.pad(jnp.concatenate([w_mid.T, w_out], axis=1), ((0, 0), (0, hidden_share - out_share))),
    )
    both_tables, from_z, projected = together(both_tables, from_z, projected)
    gate_by_z = jnp.sum(
        jnp.sum(from_z[:, in_rows : in_rows + 6].astype(f32), axis=0).reshape(2, 2, model_share),
        axis=0,
    )
    gate_by_z = lax.all_gather(gate_by_z, TENSOR, axis=1, tiled=True)
    gate_rows = pad_to(
        halves(gate_by_z).transpose(1, 0, 2).reshape(2, 12, hidden_share), (2, 16, hidden_share)
    )
    rows_by_z = 8 * in_rows
    from_xy = exchange(
        jnp.concatenate(
            [
                jnp.broadcast_to(
                    from_z[:, :in_rows].reshape(1, rows_by_z, hidden_share),
                    (8, rows_by_z, hidden_share),
                ),
                jnp.repeat(gate_rows, 4, axis=0),
            ],
            axis=1,
        ),
        ("xl", "y"),
    )
    gate_all = jnp.sum(
        jnp.sum(from_xy[:, rows_by_z : rows_by_z + 12].astype(f32), axis=0).reshape(
            2, 4 * model_share
        ),
        axis=0,
        keepdims=True,
    )
    gate_cols = lax.dynamic_slice_in_dim(gate_all, tensor_index * model_share, model_share, 1)
    in_table = (
        from_xy[:, :rows_by_z]
        .reshape(2, 4, 8, in_rows, hidden_share)
        .transpose(0, 2, 1, 3, 4)
        .reshape(64 * in_rows, hidden_share)
    )
    mid_turned = gather_z(both_tables[..., :hidden_share], hidden_share)
    out_table = gather_z(both_tables[..., hidden_share:], out_share)

    def own_cols(values):
        return lax.dynamic_slice_in_dim(values, enc_start, enc_share, values.ndim - 1)

    gain, bias = own_cols(enc_gain), own_cols(enc_bias)
    stream = own_cols(enc_stream).astype(f32) + own_cols(layer_scale) * projected
    local_mean = jnp.mean(stream, axis=1)
    local = stream - local_mean[:, None]
    gained = gain * local
    moments = jnp.stack(
        [
            local_mean,
            jnp.sum(local * local, axis=1),
            jnp.sum(gained * gained, axis=1),
            jnp.sum(gained * gain, axis=1),
            jnp.sum(gained * bias, axis=1),
        ]
    )

    block_out = (hidden.astype(jnp.float32) + gate_all * branch.astype(jnp.float32)).astype(
        jnp.bfloat16
    )
    pre_one = jnp.dot(block_out, in_table, preferred_element_type=jnp.float32)
    act_one = jax.nn.silu(pre_one).astype(jnp.bfloat16)
    shared = jnp.stack([moments] + peers(moments, TENSOR))
    sharer = tensor_index ^ jnp.arange(4, dtype=jnp.int32)

    def share_sums(values):
        return jnp.take(jnp.sum(values.reshape(4, enc_share), axis=1), sharer)[:, None]

    means = shared[:, 0]
    centre = jnp.mean(means, axis=0)
    offs = means - centre
    variance = (jnp.sum(shared[:, 1], axis=0) + enc_share * jnp.sum(offs * offs, axis=0)) / enc_width
    rstd = lax.rsqrt(variance + eps_norm)
    quad = jnp.sum(
        shared[:, 2] + offs * (2.0 * shared[:, 3] + offs * share_sums(enc_gain * enc_gain)), axis=0
    )
    cross = jnp.sum(shared[:, 4] + offs * share_sums(enc_gain * enc_bias), axis=0)
    length = rstd * (rstd * quad + 2.0 * cross) + jnp.sum(enc_bias * enc_bias)
    normed = (stream - centre[:, None]) * rstd[:, None] * gain + bias
    own_unit = (normed * lax.rsqrt(jnp.maximum(length, 0.0) + eps_norm)[:, None]).astype(bf16)
    pre_two = tensor_scatter(
        lambda t: contract_cols(act_one, row_block(mid_turned, t))
    )
    received = lax.all_to_all(own_unit, DP, split_axis=0, concat_axis=0, tiled=True)
    aligned = jnp.take(received, patch_index, axis=0).astype(jnp.float32)
    act_two = tensor_gather(jax.nn.silu(pre_two).astype(jnp.bfloat16))
    proj_out = jnp.dot(act_two, out_table, preferred_element_type=jnp.float32)
    square_sum, inner_sum = lax.psum(
        (jnp.sum(proj_out * proj_out, axis=1), jnp.sum(proj_out * aligned, axis=1)), TENSOR
    )
    inv_len = lax.rsqrt(square_sum + eps_norm)[:, None]
    inner_col = inner_sum[:, None]
    d_out = (
        -loss_scale * (aligned * inv_len - inner_col * inv_len * inv_len * inv_len * proj_out)
    ).astype(jnp.bfloat16)

    grad_out, d_out = together(contract_rows(act_two, d_out).astype(bf16), d_out)
    out_by_z = scatter_z(grad_out)
    back = tensor_scatter(lambda t: contract_cols(d_out, row_block(out_table, t)))
    d_two = tensor_gather((back * silu_slope(pre_two)).astype(jnp.bfloat16))
    mid_parts, d_two = together(xy_parts(contract_rows(d_two, act_one).astype(bf16)), d_two)
    mid_by_xy = exchange_sum(mid_parts, ("xl", "y")).astype(bf16)
    d_one = (
        jnp.dot(d_two, mid_turned, preferred_element_type=jnp.float32) * silu_slope(pre_one)
    ).astype(jnp.bfloat16)
    in_by_z = scatter_z(contract_rows(block_out, d_one).astype(bf16))
    stream_share = tensor_scatter(
        lambda t: contract_cols(d_one, row_block(in_table, t))
    )
    total_grad = up_grad.astype(jnp.float32) + stream_share
    grad_hidden = total_grad.astype(jnp.bfloat16)
    grad_branch = (gate_cols * total_grad).astype(jnp.bfloat16)
    branch_cols = lax.dynamic_slice_in_dim(
        branch, tensor_index * model_share, model_share, 1
    ).astype(jnp.float32)
    device_sum = jnp.sum(total_grad * branch_cols, axis=0)
    mid_rows = mid_by_xy.shape[1]
    sum_rows = pad_to(halves(device_sum).reshape(3, hidden_share), (16, hidden_share))
    last_z = exchange(
        jnp.concatenate(
            [mid_by_xy, jnp.broadcast_to(sum_rows[None], (8, 16, hidden_share))], axis=1
        ),
        "z",
    )
    grad_w_mid = jnp.sum(last_z[:, :mid_rows].astype(f32), axis=0).T
    sums_by_z = jnp.sum(
        last_z[:, mid_rows : mid_rows + 3].astype(f32).reshape(2, 4, 2, model_share), axis=(1, 2)
    )
    sum_rows = pad_to(halves(sums_by_z).reshape(6, hidden_share), (16, hidden_share))
    last_xy = exchange(
        jnp.concatenate(
            [
                in_by_z,
                jnp.broadcast_to(sum_rows[None], (8, 16, hidden_share)),
                pad_to(out_by_z, (8, out_by_z.shape[1], hidden_share)),
            ],
            axis=1,
        ),
        ("xl", "y"),
    )
    grad_w_in = jnp.sum(last_xy[:, :in_rows].astype(f32), axis=0)
    grad_w_out = jnp.sum(last_xy[:, in_rows + 16 :, :out_share].astype(f32), axis=0)
    image_sums = jnp.sum(
        last_xy[:, in_rows : in_rows + 6].astype(f32).reshape(2, 4, 2, 2, model_share),
        axis=(1, 2),
    ).reshape(image_count, model_share)
    grad_w_gate = lax.dot_general(
        own_emb_cols.astype(jnp.float32),
        image_sums,
        (((0,), (0,)), ((), ())),
        precision=lax.Precision.HIGHEST,
        preferred_element_type=jnp.float32,
    )
    return (grad_hidden, grad_branch, grad_w_gate, grad_w_in, grad_w_mid, grad_w_out)


def solution(mesh):
    split = Mesh(mesh.devices.reshape(2, 8, 4, 2, 2), DP + TENSOR)
    return jax.shard_map(
        body,
        mesh=split,
        in_specs=(
            P(DP, None),
            P(DP, None),
            P(DP, TENSOR),
            P(),
            P(),
            P(DP, TENSOR),
            P(DP, TENSOR),
            P(TENSOR, DP),
            P(DP, TENSOR),
            P(DP, None),
            P(DP, TENSOR),
            P(TENSOR, None),
            P(),
            P(),
            P(),
            P(DP),
        ),
        out_specs=(
            P(DP, TENSOR),
            P(DP, TENSOR),
            P(DP, TENSOR),
            P(DP, TENSOR),
            P(TENSOR, DP),
            P(DP, TENSOR),
        ),
        check_vma=False,
    )
```
